32 devices in a mesh: grp: 2 (over x), view: 4 (over y, core), slab: 4 (over z).
Axes of the slice: x: 2, y: 2, z: 4, core: 2. Of those that a mesh axis runs over, the one named last changes fastest.
Arguments:
- volume: float32 [16, 512, 512], P(('grp', 'slab'), 'view'), parts along dimension 0, may hold values from 0 to 2
- measured: float32 [8, 1024, 128], P(('grp', 'view')), parts along dimension 0, may hold values from -6 to 6
- weights: float32 [8, 1024, 128], P(('grp', 'view')), parts along dimension 0, may hold values from 0.25 to 4
- templates: bfloat16 [8, 64, 128], replicated, may hold values from -0.078125 to 0.078125
- pixel_rows: int32 [4, 65536], P('view', 'slab'), may hold values from 0 to 1023, as said below
- voxel_cols: int32 [4, 65536], P('view', 'slab'), may hold values from 0 to 32767, as said below
- template_ids: int32 [4, 65536], P('view', 'slab'), may hold values from 0 to 7
- curvature: float32 [16, 512, 512], P(('grp', 'slab'), 'view'), parts along dimension 0, may hold values from 1 to 4
Outputs:
- updated: float32 [16, 512, 512], P(('grp', 'slab'), 'view'), parts along dimension 0
The draws below stay inside these ranges and needn't reach their ends.
There are 2 independent parts, one for each index of `grp`. The reference program is written for one: setup_inputs(seed, part) draws one part's arguments, and reference() takes and returns one part's arrays. A program takes and returns all parts, laid end to end along the dimension named above; an argument that names none is the same for every part. Nothing has to cross between parts.
Inputs may be any that keep to these rules, and one draw needn't show every extreme that they name: `voxel_cols`: A view's list is made of groups of 512 consecutive entries; entry k lies in group q = k // 512 and names a voxel block of z-slab k // 16384, one of the blocks q * 256 to (q + 1) * 256 - 1; in every group the first 256 entries name each of these blocks once. `pixel_rows`: entry k, in group q = k // 512 and with w = (q % 32) % 8, names a pixel block of w * 128 to (w + 1) * 128 - 1; in every group the first 128 entries name each of these once.
All inputs are finite; a program needn't handle non-finite values.
Results may differ from the reference program's by a relative error of at most 0.0023.
Values may be sent and summed in bfloat16 or wider, within the bound.
A program may use at most 192 MiB of HBM per device.

```python
import math
import jax
import jax.numpy as jnp
from jax import lax

NX = 512
NY = 512
VOXBLK = 64
PIXBLK = 128
NTEMPL = 8
NZ = 8
VIEWS = 4
PB = 1024
SLAB_BLOCKS = 8192
ENTRIES = 16384
VWIN = 256
EGRP = 512
PWIN = 128
N_SLAB = 4


def group_entries(key, span, shape_lead):
    count = 1
    for item in shape_lead:
        count = count * item
    keys = jax.random.split(key, count + 1)
    firsts = jax.vmap(lambda one_key: jax.random.permutation(one_key, span))(keys[:count])
    rests = jax.random.randint(keys[count], (count, EGRP - span), 0, span)
    merged = jnp.concatenate([firsts.astype(jnp.int32), rests.astype(jnp.int32)], axis=1)
    return merged.reshape(tuple(shape_lead) + (EGRP,))


def draw_voxel_cols(key, part):
    key = jax.random.fold_in(key, 7)
    groups = SLAB_BLOCKS // VWIN
    local_ids = group_entries(key, VWIN, (VIEWS, N_SLAB, groups))
    group_base = (jnp.arange(groups, dtype=jnp.int32) * VWIN)[None, None, :, None]
    slab_base = (jnp.arange(N_SLAB, dtype=jnp.int32) * SLAB_BLOCKS)[None, :, None, None]
    return (local_ids + group_base + slab_base).reshape(VIEWS, N_SLAB * ENTRIES).astype(jnp.int32)


def draw_pixel_rows(key, part):
    key = jax.random.fold_in(key, 11)
    groups = SLAB_BLOCKS // VWIN
    windows = PB // PWIN
    local_ids = group_entries(key, PWIN, (VIEWS, N_SLAB, groups))
    window_base = (jnp.arange(groups, dtype=jnp.int32) % windows * PWIN)[None, None, :, None]
    return (local_ids + window_base).reshape(VIEWS, N_SLAB * ENTRIES).astype(jnp.int32)


def plant(drawn, key, low, largest):
    longest = drawn.shape.index(max(drawn.shape))
    spots = []
    for shift in (0, 1):
        where = [jax.random.randint(jax.random.fold_in(key, axis), (), 0, length) for axis, length in enumerate(drawn.shape)]
        where[longest] = (where[longest] + shift) % drawn.shape[longest]
        spots.append(tuple(where))
    return drawn.at[spots[0]].set(low).at[spots[1]].set(largest)


def shard_levels(key, dims, cuts, least, high):
    def one(axis_at, shards_of):
        heights = jax.random.uniform(jax.random.fold_in(jax.random.fold_in(key, 6), axis_at), (shards_of,), jnp.float32, least / len(cuts), high / len(cuts))
        return jnp.repeat(jnp.exp(heights), dims[axis_at] // shards_of).reshape((-1,) + (1,) * (len(dims) - axis_at - 1))

    loudness = one(*cuts[0])
    for cut in cuts[1:]:
        loudness = loudness * one(*cut)
    return loudness


def bell_draw(own_key, dims, scale, bound, cuts=(), kind=jnp.bfloat16):
    drawn = jax.random.normal(own_key, dims, jnp.float32) * scale
    if len(cuts) > 0:
        drawn = shard_levels(own_key, dims, cuts, -0.22, 0.18) * drawn
    return jnp.clip(drawn, min=-bound, max=bound).astype(kind)


def setup_inputs(seed: int = 0, part: int = 0) -> dict:
    key_list = jax.random.split(jax.random.key(seed), 9)
    part_keys = jax.random.split(jax.random.fold_in(key_list[8], part), 9)
    volume = jnp.clip(2.0 * jax.random.uniform(part_keys[0], (NZ, NY, NX), jnp.float32) ** shard_levels(part_keys[0], (NZ, NY, NX), ((0, 4), (1, 4)), -0.2, 0.2), 0.0, 2.0)
    measured = bell_draw(part_keys[1], (VIEWS, PB, PIXBLK), 1.0, 6.0, ((0, 4),), jnp.float32)
    weights = jnp.clip(jnp.exp(math.log(4.0) - 2.7725887 * jax.random.uniform(part_keys[2], (VIEWS, PB, PIXBLK), jnp.float32) ** shard_levels(part_keys[2], (VIEWS, PB, PIXBLK), ((0, 4),), -0.2, 0.2)), 0.25, 4.0)
    templates = bell_draw(key_list[3], (NTEMPL, VOXBLK, PIXBLK), (N_SLAB * ENTRIES * VOXBLK * 4 // (3 * PB)) ** -0.5, 0.078125)
    pixel_rows = draw_pixel_rows(jax.random.fold_in(key_list[8], 71), part)
    voxel_cols = draw_voxel_cols(jax.random.fold_in(key_list[8], 71), part)
    template_ids = plant(jax.random.randint(key_list[6], (VIEWS, N_SLAB * ENTRIES), 0, NTEMPL), jax.random.fold_in(key_list[6], 1), 0, NTEMPL - 1).astype(jnp.int32)
    curvature = jnp.clip(jnp.exp(math.log(4.0) - 1.3862944 * jax.random.uniform(part_keys[7], (NZ, NY, NX), jnp.float32) ** shard_levels(part_keys[7], (NZ, NY, NX), ((0, 4), (1, 4)), -0.2, 0.2)), 1.0, 4.0)
    return {"volume": volume, "measured": measured, "weights": weights, "templates": templates, "pixel_rows": pixel_rows, "voxel_cols": voxel_cols, "template_ids": template_ids, "curvature": curvature}


prior_weight = 0.25


def potential_slope(gap_value):
    power_term = jnp.power(jnp.abs(gap_value), 0.8)
    return gap_value / (1.0 + power_term) * (2.0 - 0.8 * power_term / (1.0 + power_term))


def prior_gradient(field):
    result = jnp.zeros_like(field)
    for axis_index in range(3):
        length = field.shape[axis_index]
        lower = lax.slice_in_dim(field, 0, length - 1, axis=axis_index)
        higher = lax.slice_in_dim(field, 1, length, axis=axis_index)
        slope = potential_slope(lower - higher)
        pad_low = [(0, 0), (0, 0), (0, 0)]
        pad_low[axis_index] = (0, 1)
        pad_high = [(0, 0), (0, 0), (0, 0)]
        pad_high[axis_index] = (1, 0)
        result = result + jnp.pad(slope, pad_low) + jnp.pad(-slope, pad_high)
    return result


def reference(volume, measured, weights, templates, pixel_rows, voxel_cols, template_ids, curvature):
    vol_blocks = volume.astype(jnp.bfloat16).astype(jnp.float32).reshape(-1, VOXBLK)
    table_full = templates.astype(jnp.float32)

    def one_view(back_carry, input_arrays):
        measurement_for_view, weight_for_view, row_slice_for_view, column_slice_for_view, kind_slice_for_view = input_arrays
        row_slice_for_view = row_slice_for_view.astype(jnp.int32)
        column_slice_for_view = column_slice_for_view.astype(jnp.int32)
        blocks = vol_blocks[column_slice_for_view]
        contrib = jnp.zeros((blocks.shape[0], PIXBLK), jnp.float32)
        for kind_index in range(NTEMPL):
            kind_mask = (kind_slice_for_view == kind_index).astype(jnp.float32)[:, None]
            contrib = contrib + jnp.dot(blocks * kind_mask, table_full[kind_index], precision=lax.Precision.HIGHEST)
        forward_projection = jnp.zeros((PB, PIXBLK), jnp.float32).at[row_slice_for_view].add(contrib)
        weighted_residual = (weight_for_view * (measurement_for_view - forward_projection)).astype(jnp.bfloat16)
        resid_rows = weighted_residual.astype(jnp.float32)[row_slice_for_view]
        spread = jnp.zeros((blocks.shape[0], VOXBLK), jnp.float32)
        for kind_index in range(NTEMPL):
            kind_mask = (kind_slice_for_view == kind_index).astype(jnp.float32)[:, None]
            spread = spread + jnp.dot(resid_rows * kind_mask, table_full[kind_index].T, precision=lax.Precision.HIGHEST)
        back_carry = back_carry.at[column_slice_for_view].add(spread)
        return back_carry, None

    start_back = jnp.zeros((NZ * NY * NX // VOXBLK, VOXBLK), jnp.float32)
    backproj, _ = lax.scan(one_view, start_back, (measured, weights, pixel_rows, voxel_cols, template_ids))
    backproj = backproj.reshape(NZ, NY, NX)
    prior_pull = prior_gradient(volume)
    return volume + (backproj - prior_weight * prior_pull) / curvature
```

```python
import functools

import jax
import jax.numpy as jnp
from jax import lax
from jax.experimental import pallas as pl
from jax.experimental.pallas import tpu as pltpu
from jax.sharding import PartitionSpec as P

prior_weight = 0.25
MESH = pl.DeviceIdType.MESH
f32 = jnp.float32
bf16 = jnp.bfloat16
NT = (((1,), (1,)), ((), ()))


def slope(gap):
    power = jnp.exp(0.8 * jnp.log(jnp.maximum(jnp.abs(gap), 1e-37)))
    inverse = 1.0 / (1.0 + power)
    return gap * inverse * (2.0 - 0.8 * power * inverse)


def two_terms(value):
    high = value.astype(bf16)
    return high, (value - high.astype(f32)).astype(bf16)


def kernel(
    dims,
    vol_ref, meas_ref, wt_ref, t_ref, row_ref, col_ref, kind_ref, curv_ref,
    out_ref,
    vol_t, part, r_recv, l_recv, r_send, l_send, resid_t, back, sib_in, y_in,
    z_send, z_lo, z_hi, y_lo, y_hi, prior,
    gs_sib, gs_y, gs_relay, g_recv, hz_s, hz_r, hy_s, hy_r,
    rs_s, rs_r, ls_s, ls_r, bs_s, bs_r, by_s, by_r,
):
    vc, sc, z_local, y_own, chunk_rows, kinds, vw, windows, ypg, group = dims
    ny = y_own // chunk_rows
    nych = vc // 2
    me = lax.axis_index("view")
    slab = lax.axis_index("slab")
    y = me // 2
    c = me % 2
    sib = y * 2 + 1 - c

    def remote(src, dst, ss, rs, **where):
        return pltpu.make_async_remote_copy(
            src_ref=src, dst_ref=dst, send_sem=ss, recv_sem=rs,
            device_id=where, device_id_type=MESH,
        )

    barrier = pltpu.get_barrier_semaphore()

    def greet(**where):
        pl.semaphore_signal(barrier, inc=1, device_id=where, device_id_type=MESH)

    for ref in (r_recv, l_recv, z_lo, z_hi, y_lo, y_hi):
        ref[...] = jnp.zeros_like(ref)
    greet(view=sib)
    for dy in range(1, nych):
        greet(view=lax.rem(y + dy, nych) * 2 + c)
    has_left, has_right = slab > 0, slab < sc - 1
    has_low, has_high = me > 0, me < vc - 1
    pl.when(has_left)(lambda: greet(slab=slab - 1))
    pl.when(has_right)(lambda: greet(slab=slab + 1))
    pl.when(has_low)(lambda: greet(view=me - 1))
    pl.when(has_high)(lambda: greet(view=me + 1))

    for z in range(z_local):
        for ch in range(ny):
            rows = vol_ref[z, pl.ds(ch * chunk_rows, chunk_rows), :]
            tall = jnp.concatenate([rows[:, k * 128:(k + 1) * 128] for k in range(4)], axis=0)
            turned = tall.T
            vol_t[me, z * ny + ch] = jnp.concatenate(
                [turned[:vw], turned[vw:]], axis=1
            ).astype(bf16)
    z_send[0] = vol_ref[0].astype(bf16)
    z_send[1] = vol_ref[z_local - 1].astype(bf16)

    pl.semaphore_wait(
        barrier,
        nych + jnp.where(has_left, 1, 0) + jnp.where(has_right, 1, 0)
        + jnp.where(has_low, 1, 0) + jnp.where(has_high, 1, 0),
    )

    def gather_y(dy):
        other = lax.rem(y + dy, nych)
        return remote(vol_t.at[me], vol_t.at[me], gs_y.at[dy], g_recv.at[me], view=other * 2 + c)

    gather_sib = remote(vol_t.at[me], vol_t.at[me], gs_sib, g_recv.at[me], view=sib)
    for dy in range(1, nych):
        gather_y(dy).start()
    gather_sib.start()

    z_down = remote(z_send.at[0], z_hi, hz_s.at[0], hz_r.at[0], slab=slab - 1)
    z_up = remote(z_send.at[1], z_lo, hz_s.at[1], hz_r.at[1], slab=slab + 1)
    y_down = remote(vol_ref.at[:, 0:8], y_hi, hy_s.at[0], hy_r.at[0], view=me - 1)
    y_up = remote(vol_ref.at[:, y_own - 8:y_own], y_lo, hy_s.at[1], hy_r.at[1], view=me + 1)
    pl.when(has_left)(z_down.start)
    pl.when(has_right)(z_up.start)
    pl.when(has_low)(y_down.start)
    pl.when(has_high)(y_up.start)

    vox_count = chunk_rows * 8
    pix = meas_ref.shape[1] // windows
    vox_iota = lax.broadcasted_iota(jnp.int32, (vox_count, group), 0)
    pix_iota = lax.broadcasted_iota(jnp.int32, (pix, group), 0)

    def entries(q):
        here = pl.ds(pl.multiple_of(q * group, group), group)
        col = col_ref[:, here] & (vox_count - 1)
        spot = (col & 1) * (vox_count // 2) + ((col >> 1) & 3) * chunk_rows + (col >> 3)
        return row_ref[:, here] & (pix - 1), spot, kind_ref[:, here]

    def one_hot(iota, spot):
        return jnp.where(iota == spot, 1.0, 0.0).astype(bf16)

    def relay(o):
        return remote(vol_t.at[o], vol_t.at[o], gs_relay.at[o // 2], g_recv.at[o], view=sib)

    def forward(w, k):
        yc = w + windows * k
        owner = yc // ny
        ch = yc % ny

        @pl.when((ch == 0) & (owner != me))
        def _():
            relay(owner).wait_recv()

        @pl.when((ch == 0) & (owner % 2 == c) & (owner // 2 != y))
        def _():
            relay(owner).start()

        total = None
        for z in range(z_local):
            rows, spots, kind = entries(z * ypg + yc)
            picked = jnp.dot(
                vol_t[owner, z * ny + ch], one_hot(vox_iota, spots), preferred_element_type=f32
            )
            spread = jnp.concatenate(
                [jnp.where(kind == t, picked, 0.0).astype(bf16) for t in range(kinds)], axis=0
            )
            added = lax.dot_general(
                one_hot(pix_iota, rows), spread, NT, preferred_element_type=f32
            )
            total = added if total is None else total + added
        high, rest = two_terms(total)
        return jnp.dot(high, t_ref[...], preferred_element_type=f32) + jnp.dot(
            rest, t_ref[...], preferred_element_type=f32
        )

    nk = ypg // windows
    k_base = (2 * y * ny) // windows

    def order(i):
        return lax.rem(i + c * ny, windows)

    for p in range(nk - 1):
        def pass_step(i, carry, p=p):
            w = order(i)
            value = forward(w, lax.rem(k_base + p, nk))
            if p == 0:
                part[w] = value
            else:
                part[w] = part[w] + value
            return carry
        lax.fori_loop(0, windows, pass_step, 0)

    def right_copy(i):
        return remote(r_send.at[i], r_recv.at[i], rs_s.at[i], rs_r.at[i], slab=slab + 1)

    def left_copy(i):
        return remote(l_send.at[i], l_recv.at[i], ls_s.at[i], ls_r.at[i], slab=slab - 1)

    def streams(i):
        ri = i - slab
        li = i - (sc - 1 - slab)

        @pl.when((ri >= 0) & (ri < windows))
        def _():
            pl.when(has_left)(lambda: right_copy(ri).wait_recv())

            @pl.when(has_right)
            def _():
                r_send[ri] = part[order(ri)] + r_recv[ri]
                right_copy(ri).start()

        @pl.when((li >= 0) & (li < windows))
        def _():
            pl.when(has_right)(lambda: left_copy(li).wait_recv())

            @pl.when(has_left)
            def _():
                l_send[li] = part[order(li)] + l_recv[li]
                left_copy(li).start()

    def last_step(i, carry):
        w = order(i)
        value = forward(w, lax.rem(k_base + nk - 1, nk))
        if nk > 1:
            value = part[w] + value
        part[w] = value
        streams(i)
        return carry

    lax.fori_loop(0, windows, last_step, 0)

    def tail_step(i, carry):
        streams(i)
        return carry

    lax.fori_loop(windows, windows + sc - 1, tail_step, 0)

    def resid_step(i, carry):
        w = order(i)
        here = pl.ds(pl.multiple_of(w * pix, pix), pix)
        proj = part[w] + r_recv[i] + l_recv[i]
        resid = (wt_ref[0, here, :] * (meas_ref[0, here, :] - proj)).astype(bf16)
        turned = lax.dot_general(t_ref[...], resid, NT, preferred_element_type=f32)
        resid_t[w] = jnp.concatenate(two_terms(turned), axis=1)
        return carry

    lax.fori_loop(0, windows, resid_step, 0)

    def backward(owner):
        def step(ch, carry):
            yc = owner * ny + ch
            w = lax.rem(yc, windows)
            for z in range(z_local):
                rows, spots, kind = entries(z * ypg + yc)
                chosen = one_hot(pix_iota, rows)
                wide = jnp.dot(
                    resid_t[w], jnp.concatenate([chosen, chosen], axis=0),
                    preferred_element_type=f32,
                )
                picked = wide[:vw]
                for t in range(1, kinds):
                    picked = jnp.where(kind == t, wide[t * vw:(t + 1) * vw], picked)
                added = lax.dot_general(
                    jnp.concatenate(two_terms(picked), axis=0), one_hot(vox_iota, spots), NT,
                    preferred_element_type=f32,
                )
                back[owner, z * ny + ch] = (added[:vw] + added[vw:]).astype(bf16)
            return carry
        lax.fori_loop(0, ny, step, 0)

    def to_sib(yy):
        return remote(
            back.at[yy * 2 + 1 - c], sib_in.at[yy], bs_s.at[yy], bs_r.at[yy], view=sib
        )

    def to_y(yy):
        return remote(back.at[yy * 2 + c], y_in.at[y], by_s.at[yy], by_r.at[y], view=yy * 2 + c)

    def from_y(yy):
        return remote(back.at[yy * 2 + c], y_in.at[yy], by_s.at[yy], by_r.at[yy], view=yy * 2 + c)

    def far(dy, carry):
        yy = lax.rem(y + dy, nych)
        backward(yy * 2 + 1 - c)
        to_sib(yy).start()
        backward(yy * 2 + c)
        to_sib(yy).wait_recv()
        mine = yy * 2 + c
        back[mine] = (back[mine].astype(f32) + sib_in[yy].astype(f32)).astype(bf16)
        to_y(yy).start()
        return carry

    lax.fori_loop(1, nych, far, 0)
    backward(y * 2 + 1 - c)
    to_sib(y).start()
    backward(me)

    pl.when(has_right)(z_down.wait_recv)
    pl.when(has_left)(z_up.wait_recv)
    pl.when(has_high)(y_down.wait_recv)
    pl.when(has_low)(y_up.wait_recv)
    x_width = vol_ref.shape[2]
    lane = lax.broadcasted_iota(jnp.int32, (y_own, x_width), 1)
    line = lax.broadcasted_iota(jnp.int32, (y_own, x_width), 0)
    one = lambda flag: jnp.where(flag, 1.0, 0.0)
    below = None
    for z in range(z_local):
        v = vol_ref[z]
        gx = jnp.where(lane < x_width - 1, slope(v - pltpu.roll(v, x_width - 1, 1)), 0.0)
        pull = gx - pltpu.roll(gx, 1, 1)
        top = y_hi[z, 0:1, :]
        nxt = jnp.where(line == y_own - 1, top, pltpu.roll(v, y_own - 1, 0))
        gy = slope(v - nxt) * jnp.where(line == y_own - 1, one(has_high), 1.0)
        first = slope(y_lo[z, 7:8, :] - v[0:1, :]) * one(has_low)
        pull = pull + gy - jnp.where(line == 0, first, pltpu.roll(gy, 1, 0))
        if z == 0:
            below = slope(z_lo[...].astype(f32) - v) * one(has_left)
        if z < z_local - 1:
            above = slope(v - vol_ref[z + 1])
        else:
            above = slope(v - z_hi[...].astype(f32)) * one(has_right)
        prior[z] = pull + above - below
        below = above

    to_sib(y).wait_recv()

    def wait_far(dy, carry):
        from_y(lax.rem(y + dy, nych)).wait_recv()
        return carry

    lax.fori_loop(1, nych, wait_far, 0)

    for z in range(z_local):
        for ch in range(ny):
            at = z * ny + ch
            total = back[me, at].astype(f32) + sib_in[y, at].astype(f32)
            for dy in range(1, nych):
                total = total + y_in[lax.rem(y + dy, nych), at].astype(f32)
            half = vox_count // 2
            tall = jnp.concatenate([total[:, :half], total[:, half:]], axis=0).T
            bp = jnp.concatenate(
                [tall[k * chunk_rows:(k + 1) * chunk_rows] for k in range(4)], axis=1
            )
            here = pl.ds(ch * chunk_rows, chunk_rows)
            out_ref[z, here, :] = vol_ref[z, here, :] + (
                bp - prior_weight * prior[z, here, :]
            ) / curv_ref[z, here, :]

    gather_sib.wait_send()
    for dy in range(1, nych):
        gather_y(dy).wait_send()
    pl.when(has_left)(z_down.wait_send)
    pl.when(has_right)(z_up.wait_send)
    pl.when(has_low)(y_down.wait_send)
    pl.when(has_high)(y_up.wait_send)

    def drain_y(dy, carry):
        yy = lax.rem(y + dy, nych)
        relay(yy * 2 + c).wait_send()
        to_sib(yy).wait_send()
        to_y(yy).wait_send()
        return carry

    lax.fori_loop(1, nych, drain_y, 0)
    to_sib(y).wait_send()

    def drain_z(i, carry):
        pl.when(has_right)(lambda: right_copy(i).wait_send())
        pl.when(has_left)(lambda: left_copy(i).wait_send())
        return carry

    lax.fori_loop(0, windows, drain_z, 0)


def per_device(vc, sc, volume, measured, weights, templates, rows, cols, kind_ids, curvature):
    z_local, y_own, x_width = volume.shape
    kinds, vw, pix_width = templates.shape
    group = 512
    chunk_rows = 256 // (x_width // vw)
    windows = measured.shape[1] // 128
    ypg = y_own * vc // chunk_rows
    ny = y_own // chunk_rows
    nych = vc // 2
    tile = (z_local * ny, vw, 256)
    dims = (vc, sc, z_local, y_own, chunk_rows, kinds, vw, windows, ypg, group)
    window = (windows, 128, pix_width)
    dma = pltpu.SemaphoreType.DMA
    vmem = pl.BlockSpec(memory_space=pltpu.VMEM)
    return pl.pallas_call(
        functools.partial(kernel, dims),
        out_shape=jax.ShapeDtypeStruct(volume.shape, f32),
        in_specs=[vmem] * 8,
        out_specs=vmem,
        scratch_shapes=[
            pltpu.VMEM((vc,) + tile, bf16),
            pltpu.VMEM(window, f32),
            pltpu.VMEM(window, f32),
            pltpu.VMEM(window, f32),
            pltpu.VMEM(window, f32),
            pltpu.VMEM(window, f32),
            pltpu.VMEM((windows, kinds * vw, 256), bf16),
            pltpu.VMEM((vc,) + tile, bf16),
            pltpu.VMEM((nych,) + tile, bf16),
            pltpu.VMEM((nych,) + tile, bf16),
            pltpu.VMEM((2, y_own, x_width), bf16),
            pltpu.VMEM((y_own, x_width), bf16),
            pltpu.VMEM((y_own, x_width), bf16),
            pltpu.VMEM((z_local, 8, x_width), f32),
            pltpu.VMEM((z_local, 8, x_width), f32),
            pltpu.VMEM(volume.shape, f32),
            dma, dma((nych,)), dma((nych,)), dma((vc,)),
            dma((2,)), dma((2,)), dma((2,)), dma((2,)),
            dma((windows,)), dma((windows,)), dma((windows,)), dma((windows,)),
            dma((nych,)), dma((nych,)), dma((nych,)), dma((nych,)),
        ],
        compiler_params=pltpu.CompilerParams(
            collective_id=0, has_side_effects=True, vmem_limit_bytes=40 * 1024 * 1024
        ),
    )(
        volume, measured, weights, templates.reshape(kinds * vw, pix_width),
        rows, cols, kind_ids, curvature,
    )


def solution(mesh):
    in_specs = (
        P(("grp", "slab"), "view", None),
        P(("grp", "view"), None, None),
        P(("grp", "view"), None, None),
        P(),
        P("view", "slab"),
        P("view", "slab"),
        P("view", "slab"),
        P(("grp", "slab"), "view", None),
    )
    out_specs = P(("grp", "slab"), "view", None)
    return jax.shard_map(
        functools.partial(per_device, mesh.shape["view"], mesh.shape["slab"]),
        mesh=mesh, in_specs=in_specs, out_specs=out_specs, check_vma=False,
    )
```

```python
import functools

import jax
import jax.numpy as jnp
from jax import lax
from jax.experimental import pallas as pl
from jax.experimental.pallas import tpu as pltpu
from jax.sharding import PartitionSpec as P

prior_weight = 0.25
MESH = pl.DeviceIdType.MESH
f32 = jnp.float32
bf16 = jnp.bfloat16
NT = (((1,), (1,)), ((), ()))


def slope(gap):
    power = jnp.exp(0.8 * jnp.log(jnp.maximum(jnp.abs(gap), 1e-37)))
    inverse = 1.0 / (1.0 + power)
    return gap * inverse * (2.0 - 0.8 * power * inverse)


def two_terms(value):
    high = value.astype(bf16)
    return high, (value - high.astype(f32)).astype(bf16)


def kernel(
    dims,
    vol_hbm, meas_hbm, wt_hbm, t_hbm, row_hbm, col_hbm, kind_hbm, curv_hbm,
    out_ref,
    vol_ref, meas_ref, wt_ref, t_ref, row_ref, col_ref, kind_ref, curv_ref,
    vol_t, part, r_recv, l_recv, r_send, l_send, resid_t, back, back_in,
    z_send, z_lo, z_hi, y_lo, y_hi, prior,
    gs_sib, gs_y, gs_relay, g_recv, hz_s, hz_r, hy_s, hy_r,
    rs_s, rs_r, ls_s, ls_r, b_s, b_r, load_sem,
):
    vc, sc, z_local, y_own, chunk_rows, kinds, vw, windows, ypg, group = dims
    ny = y_own // chunk_rows
    nych = vc // 2
    me = lax.axis_index("view")
    slab = lax.axis_index("slab")
    y = me // 2
    c = me % 2
    sib = y * 2 + 1 - c

    def remote(src, dst, ss, rs, **where):
        return pltpu.make_async_remote_copy(
            src_ref=src, dst_ref=dst, send_sem=ss, recv_sem=rs,
            device_id=where, device_id_type=MESH,
        )

    loads = [
        pltpu.make_async_copy(src, dst, load_sem.at[i])
        for i, (src, dst) in enumerate((
            (vol_hbm, vol_ref), (row_hbm, row_ref), (col_hbm, col_ref), (kind_hbm, kind_ref),
            (t_hbm, t_ref), (meas_hbm, meas_ref), (wt_hbm, wt_ref), (curv_hbm, curv_ref),
        ))
    ]
    for load in loads:
        load.start()

    barrier = pltpu.get_barrier_semaphore()

    def greet(**where):
        pl.semaphore_signal(barrier, inc=1, device_id=where, device_id_type=MESH)

    for ref in (r_recv, l_recv, z_lo, z_hi, y_lo, y_hi):
        ref[...] = jnp.zeros_like(ref)
    for step in range(1, vc):
        greet(view=lax.rem(me + step, vc))
    has_left, has_right = slab > 0, slab < sc - 1
    has_low, has_high = me > 0, me < vc - 1
    pl.when(has_left)(lambda: greet(slab=slab - 1))
    pl.when(has_right)(lambda: greet(slab=slab + 1))

    loads[0].wait()
    for z in range(z_local):
        for ch in range(ny):
            rows = vol_ref[z, pl.ds(ch * chunk_rows, chunk_rows), :]
            tall = jnp.concatenate([rows[:, k * 128:(k + 1) * 128] for k in range(4)], axis=0)
            turned = tall.T
            vol_t[me, z * ny + ch] = jnp.concatenate(
                [turned[:vw], turned[vw:]], axis=1
            ).astype(bf16)
    z_send[0] = vol_ref[0].astype(bf16)
    z_send[1] = vol_ref[z_local - 1].astype(bf16)

    pl.semaphore_wait(
        barrier,
        vc - 1 + jnp.where(has_left, 1, 0) + jnp.where(has_right, 1, 0),
    )

    def gather_y(dy):
        other = lax.rem(y + dy, nych)
        return remote(vol_t.at[me], vol_t.at[me], gs_y.at[dy], g_recv.at[me], view=other * 2 + c)

    gather_sib = remote(vol_t.at[me], vol_t.at[me], gs_sib, g_recv.at[me], view=sib)
    for dy in range(1, nych):
        gather_y(dy).start()
    gather_sib.start()

    z_down = remote(z_send.at[0], z_hi, hz_s.at[0], hz_r.at[0], slab=slab - 1)
    z_up = remote(z_send.at[1], z_lo, hz_s.at[1], hz_r.at[1], slab=slab + 1)
    y_down = remote(vol_ref.at[:, 0:8], y_hi, hy_s.at[0], hy_r.at[0], view=me - 1)
    y_up = remote(vol_ref.at[:, y_own - 8:y_own], y_lo, hy_s.at[1], hy_r.at[1], view=me + 1)
    pl.when(has_left)(z_down.start)
    pl.when(has_right)(z_up.start)
    pl.when(has_low)(y_down.start)
    pl.when(has_high)(y_up.start)

    for load in loads[1:5]:
        load.wait()
    vox_count = chunk_rows * 8
    pix = meas_ref.shape[1] // windows
    vox_iota = lax.broadcasted_iota(jnp.int32, (vox_count, group), 0)
    pix_iota = lax.broadcasted_iota(jnp.int32, (pix, group), 0)

    def entries(q):
        here = pl.ds(pl.multiple_of(q * group, group), group)
        col = col_ref[:, here] & (vox_count - 1)
        spot = (col & 1) * (vox_count // 2) + ((col >> 1) & 3) * chunk_rows + (col >> 3)
        return row_ref[:, here] & (pix - 1), spot, kind_ref[:, here]

    def one_hot(iota, spot):
        return jnp.where(iota == spot, 1.0, 0.0).astype(bf16)

    def relay(o):
        return remote(vol_t.at[o], vol_t.at[o], gs_relay.at[o // 2], g_recv.at[o], view=sib)

    def forward(w, k):
        yc = w + windows * k
        owner = yc // ny
        ch = yc % ny

        @pl.when((ch == 0) & (owner != me))
        def _():
            relay(owner).wait_recv()

        @pl.when((ch == 0) & (owner % 2 == c) & (owner // 2 != y))
        def _():
            relay(owner).start()

        total = None
        for z in range(z_local):
            rows, spots, kind = entries(z * ypg + yc)
            picked = jnp.dot(
                vol_t[owner, z * ny + ch], one_hot(vox_iota, spots), preferred_element_type=f32
            )
            spread = jnp.concatenate(
                [jnp.where(kind == t, picked, 0.0).astype(bf16) for t in range(kinds)], axis=0
            )
            added = lax.dot_general(
                one_hot(pix_iota, rows), spread, NT, preferred_element_type=f32
            )
            total = added if total is None else total + added
        high, rest = two_terms(total)
        return jnp.dot(high, t_ref[...], preferred_element_type=f32) + jnp.dot(
            rest, t_ref[...], preferred_element_type=f32
        )

    nk = ypg // windows
    k_base = (2 * y * ny) // windows

    def order(i):
        return lax.rem(i + c * ny, windows)

    for p in range(nk - 1):
        def pass_step(i, carry, p=p):
            w = order(i)
            value = forward(w, lax.rem(k_base + p, nk))
            if p == 0:
                part[w] = value
            else:
                part[w] = part[w] + value
            return carry
        lax.fori_loop(0, windows, pass_step, 0)

    def right_copy(i):
        return remote(r_send.at[i], r_recv.at[i], rs_s.at[i], rs_r.at[i], slab=slab + 1)

    def left_copy(i):
        return remote(l_send.at[i], l_recv.at[i], ls_s.at[i], ls_r.at[i], slab=slab - 1)

    slack = 2

    def streams(i):
        ri = i - slack * slab
        li = i - slack * (sc - 1 - slab)

        @pl.when((ri >= 0) & (ri < windows))
        def _():
            pl.when(has_left)(lambda: right_copy(ri).wait_recv())

            @pl.when(has_right)
            def _():
                r_send[ri] = part[order(ri)] + r_recv[ri]
                right_copy(ri).start()

        @pl.when((li >= 0) & (li < windows))
        def _():
            pl.when(has_right)(lambda: left_copy(li).wait_recv())

            @pl.when(has_left)
            def _():
                l_send[li] = part[order(li)] + l_recv[li]
                left_copy(li).start()

    def residual(i):
        w = order(i)
        here = pl.ds(pl.multiple_of(w * pix, pix), pix)
        proj = part[w] + r_recv[i] + l_recv[i]
        resid = (wt_ref[0, here, :] * (meas_ref[0, here, :] - proj)).astype(bf16)
        turned = lax.dot_general(t_ref[...], resid, NT, preferred_element_type=f32)
        resid_t[...] = jnp.concatenate(two_terms(turned), axis=1)

    def home(owner, ch):
        at = owner * ny + ch
        return remote(back.at[owner, ch], back_in.at[me, ch], b_s.at[at], b_r.at[me * ny + ch],
                      view=owner)

    def arrival(src, ch):
        return remote(back.at[src, ch], back_in.at[src, ch], b_s.at[src * ny + ch],
                      b_r.at[src * ny + ch], view=src)

    def backward(w, k):
        yc = w + windows * k
        owner = yc // ny
        ch = yc % ny
        for z in range(z_local):
            rows, spots, kind = entries(z * ypg + yc)
            chosen = one_hot(pix_iota, rows)
            wide = jnp.dot(
                resid_t[...], jnp.concatenate([chosen, chosen], axis=0),
                preferred_element_type=f32,
            )
            picked = wide[:vw]
            for t in range(1, kinds):
                picked = jnp.where(kind == t, wide[t * vw:(t + 1) * vw], picked)
            added = lax.dot_general(
                jnp.concatenate(two_terms(picked), axis=0), one_hot(vox_iota, spots), NT,
                preferred_element_type=f32,
            )
            back[owner, ch, z] = (added[:vw] + added[vw:]).astype(bf16)

        @pl.when(owner != me)
        def _():
            home(owner, ch).start()

    def step(i, carry, go_forward, go_back):
        if go_forward:
            w = order(i)
            value = forward(w, lax.rem(k_base + nk - 1, nk))
            if nk > 1:
                value = part[w] + value
            part[w] = value
        streams(i)
        if go_back:
            done = i - late
            residual(done)
            for k in range(nk):
                backward(order(done), lax.rem(k_base + nk - 1 + k, nk))
        return carry

    late = slack * (sc - 1)
    first, second = min(late, windows), max(late, windows)
    run = lambda lo, hi, a, b: lax.fori_loop(
        lo, hi, functools.partial(step, go_forward=a, go_back=b), 0
    )
    run(0, first, True, False)
    loads[5].wait()
    loads[6].wait()
    run(first, second, late < windows, late < windows)
    run(second, windows + late, False, True)

    pl.when(has_right)(z_down.wait_recv)
    pl.when(has_left)(z_up.wait_recv)
    pl.when(has_high)(y_down.wait_recv)
    pl.when(has_low)(y_up.wait_recv)
    x_width = vol_ref.shape[2]
    lane = lax.broadcasted_iota(jnp.int32, (y_own, x_width), 1)
    line = lax.broadcasted_iota(jnp.int32, (y_own, x_width), 0)
    one = lambda flag: jnp.where(flag, 1.0, 0.0)
    below = None
    for z in range(z_local):
        v = vol_ref[z]
        gx = jnp.where(lane < x_width - 1, slope(v - pltpu.roll(v, x_width - 1, 1)), 0.0)
        pull = gx - pltpu.roll(gx, 1, 1)
        top = y_hi[z, 0:1, :]
        nxt = jnp.where(line == y_own - 1, top, pltpu.roll(v, y_own - 1, 0))
        gy = slope(v - nxt) * jnp.where(line == y_own - 1, one(has_high), 1.0)
        first = slope(y_lo[z, 7:8, :] - v[0:1, :]) * one(has_low)
        pull = pull + gy - jnp.where(line == 0, first, pltpu.roll(gy, 1, 0))
        if z == 0:
            below = slope(z_lo[...].astype(f32) - v) * one(has_left)
        if z < z_local - 1:
            above = slope(v - vol_ref[z + 1])
        else:
            above = slope(v - z_hi[...].astype(f32)) * one(has_right)
        prior[z] = pull + above - below
        below = above

    loads[7].wait()

    def wait_back(i, carry):
        src = lax.rem(me + i // ny, vc)
        arrival(src, i % ny).wait_recv()
        return carry

    lax.fori_loop(ny, vc * ny, wait_back, 0)

    for z in range(z_local):
        for ch in range(ny):
            total = back[me, ch, z].astype(f32)
            for src in range(1, vc):
                total = total + back_in[lax.rem(me + src, vc), ch, z].astype(f32)
            half = vox_count // 2
            tall = jnp.concatenate([total[:, :half], total[:, half:]], axis=0).T
            bp = jnp.concatenate(
                [tall[k * chunk_rows:(k + 1) * chunk_rows] for k in range(4)], axis=1
            )
            here = pl.ds(ch * chunk_rows, chunk_rows)
            out_ref[z, here, :] = vol_ref[z, here, :] + (
                bp - prior_weight * prior[z, here, :]
            ) / curv_ref[z, here, :]

    gather_sib.wait_send()
    for dy in range(1, nych):
        gather_y(dy).wait_send()
    pl.when(has_left)(z_down.wait_send)
    pl.when(has_right)(z_up.wait_send)
    pl.when(has_low)(y_down.wait_send)
    pl.when(has_high)(y_up.wait_send)

    def drain_y(dy, carry):
        relay(lax.rem(y + dy, nych) * 2 + c).wait_send()
        return carry

    lax.fori_loop(1, nych, drain_y, 0)

    def drain_back(i, carry):
        home(lax.rem(me + i // ny, vc), i % ny).wait_send()
        return carry

    lax.fori_loop(ny, vc * ny, drain_back, 0)

    def drain_z(i, carry):
        pl.when(has_right)(lambda: right_copy(i).wait_send())
        pl.when(has_left)(lambda: left_copy(i).wait_send())
        return carry

    lax.fori_loop(0, windows, drain_z, 0)


def per_device(vc, sc, volume, measured, weights, templates, rows, cols, kind_ids, curvature):
    z_local, y_own, x_width = volume.shape
    kinds, vw, pix_width = templates.shape
    group = 512
    chunk_rows = 256 // (x_width // vw)
    windows = measured.shape[1] // 128
    ypg = y_own * vc // chunk_rows
    ny = y_own // chunk_rows
    nych = vc // 2
    tile = (z_local * ny, vw, 256)
    dims = (vc, sc, z_local, y_own, chunk_rows, kinds, vw, windows, ypg, group)
    window = (windows, 128, pix_width)
    dma = pltpu.SemaphoreType.DMA
    vmem = pl.BlockSpec(memory_space=pltpu.VMEM)
    flat = templates.reshape(kinds * vw, pix_width)
    args = (volume, measured, weights, flat, rows, cols, kind_ids, curvature)
    back_tile = (vc, ny, z_local, vw, 256)
    return pl.pallas_call(
        functools.partial(kernel, dims),
        out_shape=jax.ShapeDtypeStruct(volume.shape, f32),
        in_specs=[pl.BlockSpec(memory_space=pl.ANY)] * 8,
        out_specs=vmem,
        scratch_shapes=[pltpu.VMEM(arg.shape, arg.dtype) for arg in args] + [
            pltpu.VMEM((vc,) + tile, bf16),
            pltpu.VMEM(window, f32),
            pltpu.VMEM(window, f32),
            pltpu.VMEM(window, f32),
            pltpu.VMEM(window, f32),
            pltpu.VMEM(window, f32),
            pltpu.VMEM((kinds * vw, 256), bf16),
            pltpu.VMEM(back_tile, bf16),
            pltpu.VMEM(back_tile, bf16),
            pltpu.VMEM((2, y_own, x_width), bf16),
            pltpu.VMEM((y_own, x_width), bf16),
            pltpu.VMEM((y_own, x_width), bf16),
            pltpu.VMEM((z_local, 8, x_width), f32),
            pltpu.VMEM((z_local, 8, x_width), f32),
            pltpu.VMEM(volume.shape, f32),
            dma, dma((nych,)), dma((nych,)), dma((vc,)),
            dma((2,)), dma((2,)), dma((2,)), dma((2,)),
            dma((windows,)), dma((windows,)), dma((windows,)), dma((windows,)),
            dma((vc * ny,)), dma((vc * ny,)), dma((8,)),
        ],
        compiler_params=pltpu.CompilerParams(
            collective_id=0, has_side_effects=True, vmem_limit_bytes=60 * 1024 * 1024
        ),
    )(*args)


def solution(mesh):
    in_specs = (
        P(("grp", "slab"), "view", None),
        P(("grp", "view"), None, None),
        P(("grp", "view"), None, None),
        P(),
        P("view", "slab"),
        P("view", "slab"),
        P("view", "slab"),
        P(("grp", "slab"), "view", None),
    )
    out_specs = P(("grp", "slab"), "view", None)
    return jax.shard_map(
        functools.partial(per_device, mesh.shape["view"], mesh.shape["slab"]),
        mesh=mesh, in_specs=in_specs, out_specs=out_specs, check_vma=False,
    )
```

```python
import functools

import jax
import jax.numpy as jnp
from jax import lax
from jax.experimental import pallas as pl
from jax.experimental.pallas import tpu as pltpu
from jax.sharding import PartitionSpec as P

prior_weight = 0.25
MESH = pl.DeviceIdType.MESH
f32 = jnp.float32
bf16 = jnp.bfloat16
NT = (((1,), (1,)), ((), ()))


def slope(gap):
    power = jnp.exp(0.8 * jnp.log(jnp.maximum(jnp.abs(gap), 1e-37)))
    inverse = 1.0 / (1.0 + power)
    return gap * inverse * (2.0 - 0.8 * power * inverse)


def two_terms(value):
    high = value.astype(bf16)
    return high, (value - high.astype(f32)).astype(bf16)


def encode(value):
    most = jnp.max(jnp.abs(value), axis=0, keepdims=True)
    level = jnp.ceil(jnp.log2(jnp.maximum(most, 1e-30)) + 0.001)
    codes = jnp.round(value * jnp.exp2(15.0 - level))
    codes = jnp.clip(codes, -32767.0, 32767.0)
    tail = jnp.broadcast_to(level, (16, value.shape[1]))
    return jnp.concatenate([codes, tail], axis=0).astype(jnp.int32).astype(jnp.int16)


def decode(message):
    wide = message.astype(jnp.int32).astype(f32)
    return wide[:-16] * jnp.exp2(wide[-16:-15] - 15.0)


def kernel(
    dims,
    vol_hbm, meas_hbm, wt_hbm, t_hbm, row_hbm, col_hbm, kind_hbm, curv_hbm,
    out_ref,
    vol_ref, meas_ref, wt_ref, t_ref, row_ref, col_ref, kind_ref, curv_ref,
    vol_t, part, r_recv, l_recv, r_send, l_send, resid_t, back, back_in,
    z_send, z_lo, z_hi, y_lo, y_hi, prior,
    gs_sib, gs_y, gs_relay, g_recv, hz_s, hz_r, hy_s, hy_r,
    rs_s, rs_r, ls_s, ls_r, b_s, b_r, load_sem,
):
    vc, sc, z_local, y_own, chunk_rows, kinds, vw, windows, ypg, group = dims
    ny = y_own // chunk_rows
    nych = vc // 2
    me = lax.axis_index("view")
    slab = lax.axis_index("slab")
    y = me // 2
    c = me % 2
    sib = y * 2 + 1 - c

    def remote(src, dst, ss, rs, **where):
        return pltpu.make_async_remote_copy(
            src_ref=src, dst_ref=dst, send_sem=ss, recv_sem=rs,
            device_id=where, device_id_type=MESH,
        )

    loads = [
        pltpu.make_async_copy(src, dst, load_sem.at[i])
        for i, (src, dst) in enumerate((
            (vol_hbm, vol_ref), (row_hbm, row_ref), (col_hbm, col_ref), (kind_hbm, kind_ref),
            (t_hbm, t_ref), (meas_hbm, meas_ref), (wt_hbm, wt_ref), (curv_hbm, curv_ref),
        ))
    ]
    for load in loads:
        load.start()

    barrier = pltpu.get_barrier_semaphore()

    def greet(**where):
        pl.semaphore_signal(barrier, inc=1, device_id=where, device_id_type=MESH)

    for ref in (r_recv, l_recv, z_lo, z_hi, y_lo, y_hi):
        ref[...] = jnp.zeros_like(ref)
    for step in range(1, vc):
        greet(view=lax.rem(me + step, vc))
    has_left, has_right = slab > 0, slab < sc - 1
    has_low, has_high = me > 0, me < vc - 1
    pl.when(has_left)(lambda: greet(slab=slab - 1))
    pl.when(has_right)(lambda: greet(slab=slab + 1))

    loads[0].wait()
    for z in range(z_local):
        for ch in range(ny):
            rows = vol_ref[z, pl.ds(ch * chunk_rows, chunk_rows), :]
            tall = jnp.concatenate([rows[:, k * 128:(k + 1) * 128] for k in range(4)], axis=0)
            turned = tall.T
            vol_t[me, z * ny + ch] = jnp.concatenate(
                [turned[:vw], turned[vw:]], axis=1
            ).astype(bf16)
    z_send[0] = vol_ref[0].astype(bf16)
    z_send[1] = vol_ref[z_local - 1].astype(bf16)

    pl.semaphore_wait(
        barrier,
        vc - 1 + jnp.where(has_left, 1, 0) + jnp.where(has_right, 1, 0),
    )

    def gather_y(dy):
        other = lax.rem(y + dy, nych)
        return remote(vol_t.at[me], vol_t.at[me], gs_y.at[dy], g_recv.at[me], view=other * 2 + c)

    gather_sib = remote(vol_t.at[me], vol_t.at[me], gs_sib, g_recv.at[me], view=sib)
    for dy in range(1, nych):
        gather_y(dy).start()
    gather_sib.start()

    z_down = remote(z_send.at[0], z_hi, hz_s.at[0], hz_r.at[0], slab=slab - 1)
    z_up = remote(z_send.at[1], z_lo, hz_s.at[1], hz_r.at[1], slab=slab + 1)
    y_down = remote(vol_ref.at[:, 0:8], y_hi, hy_s.at[0], hy_r.at[0], view=me - 1)
    y_up = remote(vol_ref.at[:, y_own - 8:y_own], y_lo, hy_s.at[1], hy_r.at[1], view=me + 1)
    pl.when(has_left)(z_down.start)
    pl.when(has_right)(z_up.start)
    pl.when(has_low)(y_down.start)
    pl.when(has_high)(y_up.start)

    for load in loads[1:5]:
        load.wait()
    vox_count = chunk_rows * 8
    pix = meas_ref.shape[1] // windows
    vox_iota = lax.broadcasted_iota(jnp.int16, (vox_count, group), 0)
    pix_iota = lax.broadcasted_iota(jnp.int16, (pix, group), 0)

    def entries(q):
        here = pl.ds(pl.multiple_of(q * group, group), group)
        col = col_ref[:, here] & (vox_count - 1)
        spot = (col & 1) * (vox_count // 2) + ((col >> 1) & 3) * chunk_rows + (col >> 3)
        return row_ref[:, here] & (pix - 1), spot, kind_ref[:, here]

    def one_hot(iota, spot):
        return jnp.where(iota == spot.astype(jnp.int16), jnp.ones((), bf16), jnp.zeros((), bf16))

    def relay(o):
        return remote(vol_t.at[o], vol_t.at[o], gs_relay.at[o // 2], g_recv.at[o], view=sib)

    def forward(w, k):
        yc = w + windows * k
        owner = yc // ny
        ch = yc % ny

        @pl.when((ch == 0) & (owner != me))
        def _():
            relay(owner).wait_recv()

        @pl.when((ch == 0) & (owner % 2 == c) & (owner // 2 != y))
        def _():
            relay(owner).start()

        total = None
        for z in range(z_local):
            rows, spots, kind = entries(z * ypg + yc)
            picked = jnp.dot(
                vol_t[owner, z * ny + ch], one_hot(vox_iota, spots), preferred_element_type=f32
            ).astype(bf16)
            kind = jnp.broadcast_to(kind.astype(jnp.int16), picked.shape)
            none = jnp.zeros_like(picked)
            spread = jnp.concatenate(
                [jnp.where(kind == t, picked, none) for t in range(kinds)], axis=0
            )
            added = lax.dot_general(
                one_hot(pix_iota, rows), spread, NT, preferred_element_type=f32
            )
            total = added if total is None else total + added
        high, rest = two_terms(total)
        return jnp.dot(high, t_ref[...], preferred_element_type=f32) + jnp.dot(
            rest, t_ref[...], preferred_element_type=f32
        )

    nk = ypg // windows
    k_base = (2 * y * ny) // windows

    def order(i):
        return lax.rem(i + c * ny, windows)

    for p in range(nk - 1):
        def pass_step(i, carry, p=p):
            w = order(i)
            value = forward(w, lax.rem(k_base + p, nk))
            if p == 0:
                part[w] = value
            else:
                part[w] = part[w] + value
            return carry
        lax.fori_loop(0, windows, pass_step, 0)

    def right_copy(i):
        return remote(r_send.at[i], r_recv.at[i], rs_s.at[i], rs_r.at[i], slab=slab + 1)

    def left_copy(i):
        return remote(l_send.at[i], l_recv.at[i], ls_s.at[i], ls_r.at[i], slab=slab - 1)

    slack = 2

    def streams(i):
        ri = i - slack * slab
        li = i - slack * (sc - 1 - slab)

        @pl.when((ri >= 0) & (ri < windows))
        def _():
            pl.when(has_left)(lambda: right_copy(ri).wait_recv())

            @pl.when(has_right)
            def _():
                r_send[ri] = encode(part[order(ri)] + decode(r_recv[ri]))
                right_copy(ri).start()

        @pl.when((li >= 0) & (li < windows))
        def _():
            pl.when(has_right)(lambda: left_copy(li).wait_recv())

            @pl.when(has_left)
            def _():
                l_send[li] = encode(part[order(li)] + decode(l_recv[li]))
                left_copy(li).start()

    def residual(i):
        w = order(i)
        here = pl.ds(pl.multiple_of(w * pix, pix), pix)
        proj = part[w] + decode(r_recv[i]) + decode(l_recv[i])
        resid = (wt_ref[0, here, :] * (meas_ref[0, here, :] - proj)).astype(bf16)
        turned = lax.dot_general(t_ref[...], resid, NT, preferred_element_type=f32)
        resid_t[...] = jnp.concatenate(two_terms(turned), axis=1)

    def home(owner, ch):
        at = owner * ny + ch
        return remote(back.at[owner, ch], back_in.at[me, ch], b_s.at[at], b_r.at[me * ny + ch],
                      view=owner)

    def arrival(src, ch):
        return remote(back.at[src, ch], back_in.at[src, ch], b_s.at[src * ny + ch],
                      b_r.at[src * ny + ch], view=src)

    def backward(w, k):
        yc = w + windows * k
        owner = yc // ny
        ch = yc % ny
        for z in range(z_local):
            rows, spots, kind = entries(z * ypg + yc)
            chosen = one_hot(pix_iota, rows)
            wide = jnp.dot(
                resid_t[...], jnp.concatenate([chosen, chosen], axis=0),
                preferred_element_type=f32,
            )
            picked = wide[:vw]
            for t in range(1, kinds):
                picked = jnp.where(kind == t, wide[t * vw:(t + 1) * vw], picked)
            added = lax.dot_general(
                jnp.concatenate(two_terms(picked), axis=0), one_hot(vox_iota, spots), NT,
                preferred_element_type=f32,
            )
            back[owner, ch, z] = (added[:vw] + added[vw:]).astype(bf16)

        @pl.when(owner != me)
        def _():
            home(owner, ch).start()

    def step(i, carry, go_forward, go_back):
        if go_forward:
            w = order(i)
            value = forward(w, lax.rem(k_base + nk - 1, nk))
            if nk > 1:
                value = part[w] + value
            part[w] = value
        streams(i)
        if go_back:
            done = i - late
            residual(done)
            for k in range(nk):
                backward(order(done), lax.rem(k_base + nk - 1 + k, nk))
        return carry

    late = slack * (sc - 1)
    first, second = min(late, windows), max(late, windows)
    run = lambda lo, hi, a, b: lax.fori_loop(
        lo, hi, functools.partial(step, go_forward=a, go_back=b), 0
    )
    run(0, first, True, False)
    loads[5].wait()
    loads[6].wait()
    run(first, second, late < windows, late < windows)
    run(second, windows + late, False, True)

    pl.when(has_right)(z_down.wait_recv)
    pl.when(has_left)(z_up.wait_recv)
    pl.when(has_high)(y_down.wait_recv)
    pl.when(has_low)(y_up.wait_recv)
    x_width = vol_ref.shape[2]
    lane = lax.broadcasted_iota(jnp.int32, (y_own, x_width), 1)
    line = lax.broadcasted_iota(jnp.int32, (y_own, x_width), 0)
    one = lambda flag: jnp.where(flag, 1.0, 0.0)
    below = None
    for z in range(z_local):
        v = vol_ref[z]
        gx = jnp.where(lane < x_width - 1, slope(v - pltpu.roll(v, x_width - 1, 1)), 0.0)
        pull = gx - pltpu.roll(gx, 1, 1)
        top = y_hi[z, 0:1, :]
        nxt = jnp.where(line == y_own - 1, top, pltpu.roll(v, y_own - 1, 0))
        gy = slope(v - nxt) * jnp.where(line == y_own - 1, one(has_high), 1.0)
        first = slope(y_lo[z, 7:8, :] - v[0:1, :]) * one(has_low)
        pull = pull + gy - jnp.where(line == 0, first, pltpu.roll(gy, 1, 0))
        if z == 0:
            below = slope(z_lo[...].astype(f32) - v) * one(has_left)
        if z < z_local - 1:
            above = slope(v - vol_ref[z + 1])
        else:
            above = slope(v - z_hi[...].astype(f32)) * one(has_right)
        prior[z] = pull + above - below
        below = above

    loads[7].wait()

    def wait_back(i, carry):
        src = lax.rem(me + i // ny, vc)
        arrival(src, i % ny).wait_recv()
        return carry

    lax.fori_loop(ny, vc * ny, wait_back, 0)

    for z in range(z_local):
        for ch in range(ny):
            total = back[me, ch, z].astype(f32)
            for src in range(1, vc):
                total = total + back_in[lax.rem(me + src, vc), ch, z].astype(f32)
            half = vox_count // 2
            tall = jnp.concatenate([total[:, :half], total[:, half:]], axis=0).T
            bp = jnp.concatenate(
                [tall[k * chunk_rows:(k + 1) * chunk_rows] for k in range(4)], axis=1
            )
            here = pl.ds(ch * chunk_rows, chunk_rows)
            out_ref[z, here, :] = vol_ref[z, here, :] + (
                bp - prior_weight * prior[z, here, :]
            ) / curv_ref[z, here, :]

    gather_sib.wait_send()
    for dy in range(1, nych):
        gather_y(dy).wait_send()
    pl.when(has_left)(z_down.wait_send)
    pl.when(has_right)(z_up.wait_send)
    pl.when(has_low)(y_down.wait_send)
    pl.when(has_high)(y_up.wait_send)

    def drain_y(dy, carry):
        relay(lax.rem(y + dy, nych) * 2 + c).wait_send()
        return carry

    lax.fori_loop(1, nych, drain_y, 0)

    def drain_back(i, carry):
        home(lax.rem(me + i // ny, vc), i % ny).wait_send()
        return carry

    lax.fori_loop(ny, vc * ny, drain_back, 0)

    def drain_z(i, carry):
        pl.when(has_right)(lambda: right_copy(i).wait_send())
        pl.when(has_left)(lambda: left_copy(i).wait_send())
        return carry

    lax.fori_loop(0, windows, drain_z, 0)


def per_device(vc, sc, volume, measured, weights, templates, rows, cols, kind_ids, curvature):
    z_local, y_own, x_width = volume.shape
    kinds, vw, pix_width = templates.shape
    group = 512
    chunk_rows = 256 // (x_width // vw)
    windows = measured.shape[1] // 128
    ypg = y_own * vc // chunk_rows
    ny = y_own // chunk_rows
    nych = vc // 2
    tile = (z_local * ny, vw, 256)
    dims = (vc, sc, z_local, y_own, chunk_rows, kinds, vw, windows, ypg, group)
    window = (windows, 128, pix_width)
    message = (windows, 128 + 16, pix_width)
    dma = pltpu.SemaphoreType.DMA
    vmem = pl.BlockSpec(memory_space=pltpu.VMEM)
    flat = templates.reshape(kinds * vw, pix_width)
    args = (volume, measured, weights, flat, rows, cols, kind_ids, curvature)
    back_tile = (vc, ny, z_local, vw, 256)
    return pl.pallas_call(
        functools.partial(kernel, dims),
        out_shape=jax.ShapeDtypeStruct(volume.shape, f32),
        in_specs=[pl.BlockSpec(memory_space=pl.ANY)] * 8,
        out_specs=vmem,
        scratch_shapes=[pltpu.VMEM(arg.shape, arg.dtype) for arg in args] + [
            pltpu.VMEM((vc,) + tile, bf16),
            pltpu.VMEM(window, f32),
            pltpu.VMEM(message, jnp.int16),
            pltpu.VMEM(message, jnp.int16),
            pltpu.VMEM(message, jnp.int16),
            pltpu.VMEM(message, jnp.int16),
            pltpu.VMEM((kinds * vw, 256), bf16),
            pltpu.VMEM(back_tile, bf16),
            pltpu.VMEM(back_tile, bf16),
            pltpu.VMEM((2, y_own, x_width), bf16),
            pltpu.VMEM((y_own, x_width), bf16),
            pltpu.VMEM((y_own, x_width), bf16),
            pltpu.VMEM((z_local, 8, x_width), f32),
            pltpu.VMEM((z_local, 8, x_width), f32),
            pltpu.VMEM(volume.shape, f32),
            dma, dma((nych,)), dma((nych,)), dma((vc,)),
            dma((2,)), dma((2,)), dma((2,)), dma((2,)),
            dma((windows,)), dma((windows,)), dma((windows,)), dma((windows,)),
            dma((vc * ny,)), dma((vc * ny,)), dma((8,)),
        ],
        compiler_params=pltpu.CompilerParams(
            collective_id=0, has_side_effects=True, vmem_limit_bytes=60 * 1024 * 1024
        ),
    )(*args)


def solution(mesh):
    in_specs = (
        P(("grp", "slab"), "view", None),
        P(("grp", "view"), None, None),
        P(("grp", "view"), None, None),
        P(),
        P("view", "slab"),
        P("view", "slab"),
        P("view", "slab"),
        P(("grp", "slab"), "view", None),
    )
    out_specs = P(("grp", "slab"), "view", None)
    return jax.shard_map(
        functools.partial(per_device, mesh.shape["view"], mesh.shape["slab"]),
        mesh=mesh, in_specs=in_specs, out_specs=out_specs, check_vma=False,
    )
```

```python
import functools

import jax
import jax.numpy as jnp
from jax import lax
from jax.experimental import pallas as pl
from jax.experimental.pallas import tpu as pltpu
from jax.sharding import PartitionSpec as P

prior_weight = 0.25
MESH = pl.DeviceIdType.MESH
f32 = jnp.float32
bf16 = jnp.bfloat16
NT = (((1,), (1,)), ((), ()))


def slope(gap):
    power = jnp.exp(0.8 * jnp.log(jnp.maximum(jnp.abs(gap), 1e-37)))
    inverse = 1.0 / (1.0 + power)
    return gap * inverse * (2.0 - 0.8 * power * inverse)


def two_terms(value):
    high = value.astype(bf16)
    return high, (value - high.astype(f32)).astype(bf16)


def encode(value):
    most = jnp.max(jnp.abs(value), axis=0, keepdims=True)
    level = jnp.ceil(jnp.log2(jnp.maximum(most, 1e-30)) + 0.001)
    codes = jnp.round(value * jnp.exp2(15.0 - level))
    codes = jnp.clip(codes, -32767.0, 32767.0)
    tail = jnp.broadcast_to(level, (16, value.shape[1]))
    return jnp.concatenate([codes, tail], axis=0).astype(jnp.int32).astype(jnp.int16)


def decode(message):
    wide = message.astype(jnp.int32).astype(f32)
    return wide[:-16] * jnp.exp2(wide[-16:-15] - 15.0)


def kernel(
    dims,
    vol_hbm, meas_hbm, wt_hbm, t_hbm, row_hbm, col_hbm, kind_hbm, curv_hbm,
    out_ref,
    vol_ref, meas_ref, wt_ref, t_ref, row_ref, col_ref, kind_ref, curv_ref,
    vol_t, part, r_recv, l_recv, r_send, l_send, resid_t, back, back_in,
    z_send, z_lo, z_hi, y_lo, y_hi, prior,
    gs_sib, gs_y, gs_relay, g_recv, hz_s, hz_r, hy_s, hy_r,
    rs_s, rs_r, ls_s, ls_r, b_s, b_r, load_sem,
):
    vc, sc, z_local, y_own, chunk_rows, kinds, vw, windows, ypg, group = dims
    ny = y_own // chunk_rows
    nych = vc // 2
    me = lax.axis_index("view")
    slab = lax.axis_index("slab")
    y = me // 2
    c = me % 2
    sib = y * 2 + 1 - c

    def remote(src, dst, ss, rs, **where):
        return pltpu.make_async_remote_copy(
            src_ref=src, dst_ref=dst, send_sem=ss, recv_sem=rs,
            device_id=where, device_id_type=MESH,
        )

    loads = [
        pltpu.make_async_copy(src, dst, load_sem.at[i])
        for i, (src, dst) in enumerate((
            (vol_hbm, vol_ref), (row_hbm, row_ref), (col_hbm, col_ref), (kind_hbm, kind_ref),
            (t_hbm, t_ref), (meas_hbm, meas_ref), (wt_hbm, wt_ref), (curv_hbm, curv_ref),
        ))
    ]
    for load in loads:
        load.start()

    barrier = pltpu.get_barrier_semaphore()

    def greet(**where):
        pl.semaphore_signal(barrier, inc=1, device_id=where, device_id_type=MESH)

    for ref in (r_recv, l_recv, z_lo, z_hi, y_lo, y_hi):
        ref[...] = jnp.zeros_like(ref)
    for step in range(1, vc):
        greet(view=lax.rem(me + step, vc))
    has_left, has_right = slab > 0, slab < sc - 1
    has_low, has_high = me > 0, me < vc - 1
    pl.when(has_left)(lambda: greet(slab=slab - 1))
    pl.when(has_right)(lambda: greet(slab=slab + 1))

    loads[0].wait()
    for z in range(z_local):
        for ch in range(ny):
            rows = vol_ref[z, pl.ds(ch * chunk_rows, chunk_rows), :]
            tall = jnp.concatenate([rows[:, k * 128:(k + 1) * 128] for k in range(4)], axis=0)
            turned = tall.T
            vol_t[me, z * ny + ch] = jnp.concatenate(
                [turned[:vw], turned[vw:]], axis=1
            ).astype(bf16)
    z_send[0] = vol_ref[0].astype(bf16)
    z_send[1] = vol_ref[z_local - 1].astype(bf16)

    pl.semaphore_wait(
        barrier,
        vc - 1 + jnp.where(has_left, 1, 0) + jnp.where(has_right, 1, 0),
    )

    def gather_y(dy):
        other = lax.rem(y + dy, nych)
        return remote(vol_t.at[me], vol_t.at[me], gs_y.at[dy], g_recv.at[me], view=other * 2 + c)

    gather_sib = remote(vol_t.at[me], vol_t.at[me], gs_sib, g_recv.at[me], view=sib)
    for dy in range(1, nych):
        gather_y(dy).start()
    gather_sib.start()

    z_down = remote(z_send.at[0], z_hi, hz_s.at[0], hz_r.at[0], slab=slab - 1)
    z_up = remote(z_send.at[1], z_lo, hz_s.at[1], hz_r.at[1], slab=slab + 1)
    y_down = remote(vol_ref.at[:, 0:8], y_hi, hy_s.at[0], hy_r.at[0], view=me - 1)
    y_up = remote(vol_ref.at[:, y_own - 8:y_own], y_lo, hy_s.at[1], hy_r.at[1], view=me + 1)
    pl.when(has_left)(z_down.start)
    pl.when(has_right)(z_up.start)
    pl.when(has_low)(y_down.start)
    pl.when(has_high)(y_up.start)

    for load in loads[1:5]:
        load.wait()
    vox_count = chunk_rows * 8
    pix = meas_ref.shape[1] // windows
    vox_iota = lax.broadcasted_iota(jnp.int16, (vox_count, group), 0)
    pix_iota = lax.broadcasted_iota(jnp.int16, (pix, group), 0)

    def entries(q):
        here = pl.ds(pl.multiple_of(q * group, group), group)
        col = col_ref[:, here] & (vox_count - 1)
        spot = (col & 1) * (vox_count // 2) + ((col >> 1) & 3) * chunk_rows + (col >> 3)
        return row_ref[:, here] & (pix - 1), spot, kind_ref[:, here]

    def one_hot(iota, spot):
        return jnp.where(iota == spot.astype(jnp.int16), jnp.ones((), bf16), jnp.zeros((), bf16))

    def relay(o):
        return remote(vol_t.at[o], vol_t.at[o], gs_relay.at[o // 2], g_recv.at[o], view=sib)

    def forward(w, k):
        yc = w + windows * k
        owner = yc // ny
        ch = yc % ny

        @pl.when((ch == 0) & (owner != me))
        def _():
            relay(owner).wait_recv()

        @pl.when((ch == 0) & (owner % 2 == c) & (owner // 2 != y))
        def _():
            relay(owner).start()

        total = None
        for z in range(z_local):
            rows, spots, kind = entries(z * ypg + yc)
            picked = jnp.dot(
                vol_t[owner, z * ny + ch], one_hot(vox_iota, spots), preferred_element_type=f32
            ).astype(bf16)
            kind = jnp.broadcast_to(kind.astype(jnp.int16), picked.shape)
            none = jnp.zeros_like(picked)
            spread = jnp.concatenate(
                [jnp.where(kind == t, picked, none) for t in range(kinds)], axis=0
            )
            added = lax.dot_general(
                one_hot(pix_iota, rows), spread, NT, preferred_element_type=f32
            )
            total = added if total is None else total + added
        high, rest = two_terms(total)
        return jnp.dot(high, t_ref[...], preferred_element_type=f32) + jnp.dot(
            rest, t_ref[...], preferred_element_type=f32
        )

    nk = ypg // windows
    k_base = (2 * y * ny) // windows

    def order(i):
        return lax.rem(i + c * ny, windows)

    for p in range(nk - 1):
        def pass_step(i, carry, p=p):
            w = order(i)
            value = forward(w, lax.rem(k_base + p, nk))
            if p == 0:
                part[w] = value
            else:
                part[w] = part[w] + value
            return carry
        lax.fori_loop(0, windows, pass_step, 0)

    def right_copy(i):
        return remote(r_send.at[i], r_recv.at[i], rs_s.at[i], rs_r.at[i], slab=slab + 1)

    def left_copy(i):
        return remote(l_send.at[i], l_recv.at[i], ls_s.at[i], ls_r.at[i], slab=slab - 1)

    slack = 3

    def streams(i):
        ri = i - slack * slab
        li = i - slack * (sc - 1 - slab)

        @pl.when((ri >= 0) & (ri < windows))
        def _():
            pl.when(has_left)(lambda: right_copy(ri).wait_recv())

            @pl.when(has_right)
            def _():
                r_send[ri] = encode(part[order(ri)] + decode(r_recv[ri]))
                right_copy(ri).start()

        @pl.when((li >= 0) & (li < windows))
        def _():
            pl.when(has_right)(lambda: left_copy(li).wait_recv())

            @pl.when(has_left)
            def _():
                l_send[li] = encode(part[order(li)] + decode(l_recv[li]))
                left_copy(li).start()

    def residual(i):
        w = order(i)
        here = pl.ds(pl.multiple_of(w * pix, pix), pix)
        proj = part[w] + decode(r_recv[i]) + decode(l_recv[i])
        resid = (wt_ref[0, here, :] * (meas_ref[0, here, :] - proj)).astype(bf16)
        turned = lax.dot_general(t_ref[...], resid, NT, preferred_element_type=f32)
        resid_t[...] = jnp.concatenate(two_terms(turned), axis=1)

    def home(owner, ch):
        at = owner * ny + ch
        return remote(back.at[owner, ch], back_in.at[me, ch], b_s.at[at], b_r.at[me * ny + ch],
                      view=owner)

    def arrival(src, ch):
        return remote(back.at[src, ch], back_in.at[src, ch], b_s.at[src * ny + ch],
                      b_r.at[src * ny + ch], view=src)

    def backward(w, k):
        yc = w + windows * k
        owner = yc // ny
        ch = yc % ny
        for z in range(z_local):
            rows, spots, kind = entries(z * ypg + yc)
            chosen = one_hot(pix_iota, rows)
            wide = jnp.dot(
                resid_t[...], jnp.concatenate([chosen, chosen], axis=0),
                preferred_element_type=f32,
            )
            picked = wide[:vw]
            for t in range(1, kinds):
                picked = jnp.where(kind == t, wide[t * vw:(t + 1) * vw], picked)
            added = lax.dot_general(
                jnp.concatenate(two_terms(picked), axis=0), one_hot(vox_iota, spots), NT,
                preferred_element_type=f32,
            )
            back[owner, ch, z] = (added[:vw] + added[vw:]).astype(bf16)

        @pl.when(owner != me)
        def _():
            home(owner, ch).start()

    def step(i, carry, go_forward, go_back):
        if go_forward:
            w = order(i)
            value = forward(w, lax.rem(k_base + nk - 1, nk))
            if nk > 1:
                value = part[w] + value
            part[w] = value
        streams(i)
        if go_back:
            done = i - late
            residual(done)
            for k in range(nk):
                backward(order(done), lax.rem(k_base + nk - 1 + k, nk))
        return carry

    late = slack * (sc - 1)
    first, second = min(late, windows), max(late, windows)
    run = lambda lo, hi, a, b: lax.fori_loop(
        lo, hi, functools.partial(step, go_forward=a, go_back=b), 0
    )
    run(0, first, True, False)
    loads[5].wait()
    loads[6].wait()
    run(first, second, late < windows, late < windows)
    run(second, windows + late, False, True)

    pl.when(has_right)(z_down.wait_recv)
    pl.when(has_left)(z_up.wait_recv)
    pl.when(has_high)(y_down.wait_recv)
    pl.when(has_low)(y_up.wait_recv)
    x_width = vol_ref.shape[2]
    lane = lax.broadcasted_iota(jnp.int32, (y_own, x_width), 1)
    line = lax.broadcasted_iota(jnp.int32, (y_own, x_width), 0)
    one = lambda flag: jnp.where(flag, 1.0, 0.0)
    below = None
    for z in range(z_local):
        v = vol_ref[z]
        gx = jnp.where(lane < x_width - 1, slope(v - pltpu.roll(v, x_width - 1, 1)), 0.0)
        pull = gx - pltpu.roll(gx, 1, 1)
        top = y_hi[z, 0:1, :]
        nxt = jnp.where(line == y_own - 1, top, pltpu.roll(v, y_own - 1, 0))
        gy = slope(v - nxt) * jnp.where(line == y_own - 1, one(has_high), 1.0)
        first = slope(y_lo[z, 7:8, :] - v[0:1, :]) * one(has_low)
        pull = pull + gy - jnp.where(line == 0, first, pltpu.roll(gy, 1, 0))
        if z == 0:
            below = slope(z_lo[...].astype(f32) - v) * one(has_left)
        if z < z_local - 1:
            above = slope(v - vol_ref[z + 1])
        else:
            above = slope(v - z_hi[...].astype(f32)) * one(has_right)
        prior[z] = pull + above - below
        below = above

    loads[7].wait()

    for ch in range(ny):
        for src in range(1, vc):
            arrival(lax.rem(me + src, vc), ch).wait_recv()
        for z in range(z_local):
            total = back[me, ch, z].astype(f32)
            for src in range(1, vc):
                total = total + back_in[lax.rem(me + src, vc), ch, z].astype(f32)
            half = vox_count // 2
            tall = jnp.concatenate([total[:, :half], total[:, half:]], axis=0).T
            bp = jnp.concatenate(
                [tall[k * chunk_rows:(k + 1) * chunk_rows] for k in range(4)], axis=1
            )
            here = pl.ds(ch * chunk_rows, chunk_rows)
            out_ref[z, here, :] = vol_ref[z, here, :] + (
                bp - prior_weight * prior[z, here, :]
            ) / curv_ref[z, here, :]

    gather_sib.wait_send()
    for dy in range(1, nych):
        gather_y(dy).wait_send()
    pl.when(has_left)(z_down.wait_send)
    pl.when(has_right)(z_up.wait_send)
    pl.when(has_low)(y_down.wait_send)
    pl.when(has_high)(y_up.wait_send)

    def drain_y(dy, carry):
        relay(lax.rem(y + dy, nych) * 2 + c).wait_send()
        return carry

    lax.fori_loop(1, nych, drain_y, 0)

    def drain_back(i, carry):
        home(lax.rem(me + i // ny, vc), i % ny).wait_send()
        return carry

    lax.fori_loop(ny, vc * ny, drain_back, 0)

    def drain_z(i, carry):
        pl.when(has_right)(lambda: right_copy(i).wait_send())
        pl.when(has_left)(lambda: left_copy(i).wait_send())
        return carry

    lax.fori_loop(0, windows, drain_z, 0)


def per_device(vc, sc, volume, measured, weights, templates, rows, cols, kind_ids, curvature):
    z_local, y_own, x_width = volume.shape
    kinds, vw, pix_width = templates.shape
    group = 512
    chunk_rows = 256 // (x_width // vw)
    windows = measured.shape[1] // 128
    ypg = y_own * vc // chunk_rows
    ny = y_own // chunk_rows
    nych = vc // 2
    tile = (z_local * ny, vw, 256)
    dims = (vc, sc, z_local, y_own, chunk_rows, kinds, vw, windows, ypg, group)
    window = (windows, 128, pix_width)
    message = (windows, 128 + 16, pix_width)
    dma = pltpu.SemaphoreType.DMA
    vmem = pl.BlockSpec(memory_space=pltpu.VMEM)
    flat = templates.reshape(kinds * vw, pix_width)
    args = (volume, measured, weights, flat, rows, cols, kind_ids, curvature)
    back_tile = (vc, ny, z_local, vw, 256)
    return pl.pallas_call(
        functools.partial(kernel, dims),
        out_shape=jax.ShapeDtypeStruct(volume.shape, f32),
        in_specs=[pl.BlockSpec(memory_space=pl.ANY)] * 8,
        out_specs=vmem,
        scratch_shapes=[pltpu.VMEM(arg.shape, arg.dtype) for arg in args] + [
            pltpu.VMEM((vc,) + tile, bf16),
            pltpu.VMEM(window, f32),
            pltpu.VMEM(message, jnp.int16),
            pltpu.VMEM(message, jnp.int16),
            pltpu.VMEM(message, jnp.int16),
            pltpu.VMEM(message, jnp.int16),
            pltpu.VMEM((kinds * vw, 256), bf16),
            pltpu.VMEM(back_tile, bf16),
            pltpu.VMEM(back_tile, bf16),
            pltpu.VMEM((2, y_own, x_width), bf16),
            pltpu.VMEM((y_own, x_width), bf16),
            pltpu.VMEM((y_own, x_width), bf16),
            pltpu.VMEM((z_local, 8, x_width), f32),
            pltpu.VMEM((z_local, 8, x_width), f32),
            pltpu.VMEM(volume.shape, f32),
            dma, dma((nych,)), dma((nych,)), dma((vc,)),
            dma((2,)), dma((2,)), dma((2,)), dma((2,)),
            dma((windows,)), dma((windows,)), dma((windows,)), dma((windows,)),
            dma((vc * ny,)), dma((vc * ny,)), dma((8,)),
        ],
        compiler_params=pltpu.CompilerParams(
            collective_id=0, has_side_effects=True, vmem_limit_bytes=60 * 1024 * 1024
        ),
    )(*args)


def solution(mesh):
    in_specs = (
        P(("grp", "slab"), "view", None),
        P(("grp", "view"), None, None),
        P(("grp", "view"), None, None),
        P(),
        P("view", "slab"),
        P("view", "slab"),
        P("view", "slab"),
        P(("grp", "slab"), "view", None),
    )
    out_specs = P(("grp", "slab"), "view", None)
    return jax.shard_map(
        functools.partial(per_device, mesh.shape["view"], mesh.shape["slab"]),
        mesh=mesh, in_specs=in_specs, out_specs=out_specs, check_vma=False,
    )
```
